32 devices in a mesh: dp: 8 (over y, x, core), tile: 4 (over z).
Axes of the slice: x: 2, y: 2, z: 4, core: 2. Of those that a mesh axis runs over, the one named last changes fastest.
Arguments:
- vit_tokens: bfloat16 [16, 576, 1024], P('dp', 'tile'), may hold values from -6 to 6
- hires_map: bfloat16 [16, 32, 32, 1536], P('dp', 'tile'), may hold values from -6 to 6
- norm1_gain: float32 [1024], replicated, may hold values from 0.5 to 1.5
- norm1_shift: float32 [1024], replicated, may hold values from -1.75 to 1.75
- qkv_weight: bfloat16 [1024, 3072], P('dp'), may hold values from -0.1875 to 0.1875
- attn_weight: bfloat16 [1024, 1024], P('dp'), may hold values from -0.75 to 0.75
- norm2_gain: float32 [1024], replicated, may hold values from 0.5 to 1.5
- norm2_shift: float32 [1024], replicated, may hold values from -1.75 to 1.75
- vit_fc1: bfloat16 [1024, 4096], P('dp'), may hold values from -0.1875 to 0.1875
- vit_fc2: bfloat16 [4096, 1024], P('dp'), may hold values from -0.09375 to 0.09375
- conv_kernel: float32 [49, 1536], replicated, may hold values from -0.875 to 0.875
- conv_gain: float32 [1536], replicated, may hold values from 0.5 to 1.5
- conv_shift: float32 [1536], replicated, may hold values from -1.75 to 1.75
- conv_fc1: bfloat16 [1536, 6144], P('dp'), may hold values from -0.15625 to 0.15625
- conv_fc2: bfloat16 [6144, 1536], P('dp'), may hold values from -0.078125 to 0.078125
- layer_scale: float32 [1536], replicated, may hold values from 0.5 to 1.5
- adapter_weight: bfloat16 [1536, 1024], P('dp'), may hold values from -0.15625 to 0.15625
- adapter_bias: float32 [1024], replicated, may hold values from -1.75 to 1.75
- adapter_kernel: float32 [9, 1024], replicated, may hold values from -3.5 to 3.5
- adapter_gate: float32 [1024], replicated, may hold values from 0.4 to 1.2
- proj_fc1: bfloat16 [1024, 4096], P('dp'), may hold values from -0.1875 to 0.1875
- proj_bias1: float32 [4096], replicated, may hold values from -1.75 to 1.75
- proj_fc2: bfloat16 [4096, 4096], P('dp'), may hold values from -0.09375 to 0.09375
- proj_bias2: float32 [4096], replicated, may hold values from -1.75 to 1.75
- projected_cot: bfloat16 [16, 576, 4096], P('dp', 'tile'), may hold values from -6 to 6
- hires_cot: bfloat16 [16, 32, 32, 1536], P('dp', 'tile'), may hold values from -6 to 6
Outputs:
- projected: bfloat16 [16, 576, 4096], P('dp', 'tile')
- hires_out: bfloat16 [16, 32, 32, 1536], P('dp', 'tile')
- tokens_grad: float32 [16, 576, 1024], P('dp', 'tile')
- hires_grad: float32 [16, 32, 32, 1536], P('dp', 'tile')
- adapter_weight_grad: float32 [1536, 1024], P(('dp', 'tile'))
- adapter_bias_grad: float32 [1024], replicated
- adapter_kernel_grad: float32 [9, 1024], replicated
- adapter_gate_grad: float32 [1024], replicated
- proj_fc1_grad: float32 [1024, 4096], P(('dp', 'tile'))
- proj_bias1_grad: float32 [4096], replicated
- proj_fc2_grad: float32 [4096, 4096], P(('dp', 'tile'))
- proj_bias2_grad: float32 [4096], replicated
The draws below stay inside these ranges and needn't reach their ends.
All inputs are finite; a program needn't handle non-finite values.
Results may differ from the reference program's by a relative error of at most 0.014.
Values may be sent and summed in bfloat16 or wider, within the bound.
A program may use at most 384 MiB of HBM per device.

```python
import math
import jax
import jax.numpy as jnp
from jax import lax

VD = 1024
HEADS = 16
HEAD = 64
VF = 4096
CC = 1536
CF = 6144
PH = 4096
PO = 4096
GV = 24
GH = 32
IMAGES = 16


def steps_of(own_key, dims, pieces, low, largest):
    factor_of = 1.0
    for dim, blocks in pieces:
        steps = jax.random.uniform(jax.random.fold_in(jax.random.fold_in(own_key, 6), dim), (blocks,), jnp.float32, low / len(pieces), largest / len(pieces))
        factor_of = factor_of * jnp.repeat(jnp.exp(steps), dims[dim] // blocks).reshape((-1,) + (1,) * (len(dims) - 1 - dim))
    return factor_of


def gaussian(own_key, shape, scale, limit, shards=(), held_as=jnp.bfloat16):
    gain = steps_of(own_key, shape, shards, -0.22, 0.18) if shards else 1.0
    entries = jax.random.normal(own_key, shape, jnp.float32) * scale * gain
    return jnp.minimum(jnp.maximum(entries, -limit), limit).astype(held_as)


def setup_inputs(seed: int = 0) -> dict:
    splits = jax.random.split(jax.random.key(seed), 27)
    return {
        "vit_tokens": gaussian(splits[0], (IMAGES, GV * GV, VD), 1.0, 6.0, ((0, 8), (1, 4))),
        "hires_map": gaussian(splits[1], (IMAGES, GH, GH, CC), 1.0, 6.0, ((0, 8), (1, 4))),
        "norm1_gain": jnp.clip(1.0 + 0.1 * jax.random.normal(splits[2], (VD,), jnp.float32), 0.5, 1.5),
        "norm1_shift": gaussian(splits[3], (VD,), 0.3, 1.75, (), jnp.float32),
        "qkv_weight": gaussian(splits[4], (VD, 3 * VD), VD ** -0.5, 0.1875, ((0, 8),)),
        "attn_weight": gaussian(splits[5], (VD, VD), (VD // 16) ** -0.5, 0.75, ((0, 8),)),
        "norm2_gain": jnp.clip(1.0 + 0.1 * jax.random.normal(splits[6], (VD,), jnp.float32), 0.5, 1.5),
        "norm2_shift": gaussian(splits[7], (VD,), 0.3, 1.75, (), jnp.float32),
        "vit_fc1": gaussian(splits[8], (VD, VF), VD ** -0.5, 0.1875, ((0, 8),)),
        "vit_fc2": gaussian(splits[9], (VF, VD), VF ** -0.5, 0.09375, ((0, 8),)),
        "conv_kernel": gaussian(splits[10], (49, CC), 49 ** -0.5, 0.875, (), jnp.float32),
        "conv_gain": jnp.clip(1.0 + 0.1 * jax.random.normal(splits[11], (CC,), jnp.float32), 0.5, 1.5),
        "conv_shift": gaussian(splits[12], (CC,), 0.3, 1.75, (), jnp.float32),
        "conv_fc1": gaussian(splits[13], (CC, CF), CC ** -0.5, 0.15625, ((0, 8),)),
        "conv_fc2": gaussian(splits[14], (CF, CC), CF ** -0.5, 0.078125, ((0, 8),)),
        "layer_scale": jnp.clip(1.0 + 0.1 * jax.random.normal(splits[15], (CC,), jnp.float32), 0.5, 1.5),
        "adapter_weight": gaussian(splits[16], (CC, VD), CC ** -0.5, 0.15625, ((0, 8),)),
        "adapter_bias": gaussian(splits[17], (VD,), 0.3, 1.75, (), jnp.float32),
        "adapter_kernel": gaussian(splits[18], (9, VD), 3 ** -0.5, 3.5, (), jnp.float32),
        "adapter_gate": jnp.clip(jax.random.uniform(splits[19], (VD,), jnp.float32, 0.4, 1.2), 0.4, 1.2),
        "proj_fc1": gaussian(splits[20], (VD, PH), VD ** -0.5, 0.1875, ((0, 8),)),
        "proj_bias1": gaussian(splits[21], (PH,), 0.3, 1.75, (), jnp.float32),
        "proj_fc2": gaussian(splits[22], (PH, PO), PH ** -0.5, 0.09375, ((0, 8),)),
        "proj_bias2": gaussian(splits[23], (PO,), 0.3, 1.75, (), jnp.float32),
        "projected_cot": gaussian(splits[24], (IMAGES, GV * GV, PO), 1.0, 6.0, ((0, 8), (1, 4))),
        "hires_cot": gaussian(splits[25], (IMAGES, GH, GH, CC), 1.0, 6.0, ((0, 8), (1, 4))),
    }


HIGHEST_PRECISION = lax.Precision.HIGHEST

@jax.custom_vjp
def low(v):
    return lax.optimization_barrier(v.astype(jnp.bfloat16)).astype(jnp.float32)

@jax.custom_vjp
def low_back(v):
    return v

def low_keep(v):
    return (low(v), None)

def low_pass(kept, grad):
    return (grad,)

def back_keep(v):
    return (v, None)

def back_low(kept, grad):
    return (low(grad),)
low.defvjp(low_keep, low_pass)
low_back.defvjp(back_keep, back_low)

def matmul(left, right):
    return jnp.einsum('...i,ij->...j', left, right, precision=HIGHEST_PRECISION)

def layer_norm(values, norm_gain, norm_shift, epsilon):
    average = lax.optimization_barrier(jnp.mean(values, axis=-1, keepdims=True))
    centred = values - average
    spread = lax.optimization_barrier(jnp.mean(centred * centred, axis=-1, keepdims=True))
    return centred * lax.rsqrt(spread + epsilon) * norm_gain + norm_shift

def depthwise(field, kernel, reach):
    width = 2 * reach + 1
    row_count = field.shape[1]
    col_count = field.shape[2]
    padded = jnp.pad(field, ((0, 0), (reach, reach), (reach, reach), (0, 0)))
    total = jnp.zeros(field.shape, field.dtype)
    for row_off in range(width):
        for col_off in range(width):
            window = padded[:, row_off:row_off + row_count, col_off:col_off + col_count]
            total = total + window * kernel[row_off * width + col_off]
    return total

def pool_matrix(count_out, count_in):
    out_index = jnp.arange(count_out)[:, None]
    in_index = jnp.arange(count_in)[None, :]
    first_row = out_index * count_in // count_out
    end_row = ((out_index + 1) * count_in + count_out - 1) // count_out
    member = (in_index >= first_row) & (in_index < end_row)
    return member.astype(jnp.float32) / (end_row - first_row).astype(jnp.float32)

def reference(vit_tokens, hires_map, norm1_gain, norm1_shift, qkv_weight, attn_weight, norm2_gain, norm2_shift, vit_fc1, vit_fc2, conv_kernel, conv_gain, conv_shift, conv_fc1, conv_fc2, layer_scale, adapter_weight, adapter_bias, adapter_kernel, adapter_gate, proj_fc1, proj_bias1, proj_fc2, proj_bias2, projected_cot, hires_cot):
    qkv_full = qkv_weight.astype(jnp.float32)
    attn_full = attn_weight.astype(jnp.float32)
    vit_up = vit_fc1.astype(jnp.float32)
    vit_down = vit_fc2.astype(jnp.float32)
    conv_up = conv_fc1.astype(jnp.float32)
    conv_down = conv_fc2.astype(jnp.float32)
    row_pool = pool_matrix(GV, GH)
    col_pool = pool_matrix(GV, GH)
    trainable = (adapter_weight.astype(jnp.float32), adapter_bias, adapter_kernel, adapter_gate, proj_fc1.astype(jnp.float32), proj_bias1, proj_fc2.astype(jnp.float32), proj_bias2)

    def forward(tokens_in, hires_in, weights):
        wa_full, ba_vec, akernel, agate, pw_up, pb_up, pw_down, pb_down = weights
        images_here = tokens_in.shape[0]
        normed_a = low(layer_norm(tokens_in, norm1_gain, norm1_shift, 1e-05))
        qkv_all = low(low_back(matmul(normed_a, qkv_full)))
        query = qkv_all[..., :VD].reshape(images_here, -1, HEADS, HEAD)
        keys_all = qkv_all[..., VD:2 * VD].reshape(images_here, -1, HEADS, HEAD)
        values_all = qkv_all[..., 2 * VD:].reshape(images_here, -1, HEADS, HEAD)
        scores = low_back(jnp.einsum('ithe,ishe->ihts', query, keys_all, precision=HIGHEST_PRECISION) * HEAD ** (-0.5))
        probs = jax.nn.softmax(scores, axis=-1)
        attended = low(low_back(jnp.einsum('ihts,ishe->ithe', low(probs), values_all, precision=HIGHEST_PRECISION)))
        attended = attended.reshape(images_here, -1, VD)
        hidden_a = tokens_in + low_back(matmul(attended, attn_full))
        normed_b = low(layer_norm(hidden_a, norm2_gain, norm2_shift, 1e-05))
        up_a = low_back(matmul(normed_b, vit_up))
        act_a = low(jax.nn.gelu(up_a))
        vit_out = hidden_a + low_back(matmul(act_a, vit_down))
        conv_in = depthwise(hires_in, conv_kernel, 3)
        normed_c = low(layer_norm(conv_in, conv_gain, conv_shift, 1e-06))
        up_c = low_back(matmul(normed_c, conv_up))
        act_c = low(jax.nn.gelu(up_c))
        refined = hires_in + layer_scale * low_back(matmul(act_c, conv_down))
        pooled = jnp.einsum('ar,irch->iach', row_pool, refined, precision=HIGHEST_PRECISION)
        pooled = low(jnp.einsum('bc,iach->iabh', col_pool, pooled, precision=HIGHEST_PRECISION))
        adapted = low(low_back(matmul(pooled, wa_full) + ba_vec))
        mixed_map = depthwise(adapted, akernel, 1).reshape(images_here, -1, VD)
        merged = vit_out + jnp.tanh(agate) * mixed_map
        pre_act = low_back(matmul(low(merged), pw_up) + pb_up)
        act_p = low(jax.nn.gelu(pre_act))
        return (matmul(act_p, pw_down) + pb_down, refined)
    images = vit_tokens.shape[0]
    group_size = math.gcd(images, 4)
    blocks = images // group_size

    def by_blocks(array):
        return array.astype(jnp.float32).reshape((blocks, group_size) + array.shape[1:])

    def per_block(totals, block_inputs):
        tokens_blk, hires_blk, cot_tokens, cot_hires = block_inputs
        outputs, pullback = jax.vjp(forward, tokens_blk, hires_blk, trainable)
        tokens_part, hires_part, train_part = pullback((cot_tokens, cot_hires))
        totals = jax.tree.map(jnp.add, totals, train_part)
        return (totals, (outputs[0].astype(jnp.bfloat16), outputs[1].astype(jnp.bfloat16), tokens_part, hires_part))
    initial = jax.tree.map(jnp.zeros_like, trainable)
    totals, stacked = lax.scan(per_block, initial, (by_blocks(vit_tokens), by_blocks(hires_map), by_blocks(projected_cot), by_blocks(hires_cot)))
    projected = stacked[0].reshape((images,) + stacked[0].shape[2:])
    hires_out = stacked[1].reshape((images,) + stacked[1].shape[2:])
    tokens_grad = stacked[2].reshape((images,) + stacked[2].shape[2:])
    hires_grad = stacked[3].reshape((images,) + stacked[3].shape[2:])
    return (projected, hires_out, tokens_grad, hires_grad, totals[0], totals[1], totals[2], totals[3], totals[4], totals[5], totals[6], totals[7])
```

```python
import functools

import jax
import jax.numpy as jnp
from jax import lax
from jax.experimental import pallas as pl
from jax.experimental.pallas import tpu as pltpu
from jax.sharding import PartitionSpec as P

HEADS = 16
GV = 24


EPS_VIT = 1e-05
EPS_CONV = 1e-06


def padded(shard, sides, width):
    for axis, dim in sides:
        size, length = (lax.axis_size(axis), shard.shape[dim])
        up = [(i, (i + 1) % size) for i in range(size - 1)]
        down = [(j, i) for i, j in up]
        last = lax.slice_in_dim(shard, length - width, length, axis=dim)
        leading = lax.slice_in_dim(shard, 0, width, axis=dim)
        before = lax.ppermute(last, axis, up)
        after = lax.ppermute(leading, axis, down)
        shard = jnp.concatenate([before, shard, after], axis=dim)
    return shard


def layer_norm(values, norm_gain, norm_shift, epsilon):
    average = jnp.mean(values, axis=-1, keepdims=True)
    centred = values - average
    spread = jnp.mean(centred * centred, axis=-1, keepdims=True)
    return centred * lax.rsqrt(spread + epsilon) * norm_gain + norm_shift


def product(left, right):
    return jnp.dot(left, right, preferred_element_type=jnp.float32)


def times_transposed(left, right):
    return lax.dot_general(
        left, right, (((1,), (1,)), ((), ())), preferred_element_type=jnp.float32
    )


def row_contract(left, right):
    return lax.dot_general(
        left, right, (((0,), (0,)), ((), ())), preferred_element_type=jnp.float32
    )


def pool_matrix(count_out, count_in):
    out_index = jnp.arange(count_out)[:, None]
    in_index = jnp.arange(count_in)[None, :]
    first_row = out_index * count_in // count_out
    end_row = ((out_index + 1) * count_in + count_out - 1) // count_out
    member = (in_index >= first_row) & (in_index < end_row)
    return member.astype(jnp.float32) / (end_row - first_row).astype(jnp.float32)


def with_partner(values):
    return jnp.concatenate([values, exchange(values, "tile", 1)])


def depthwise_rows(framed_rows, kernel, reach):
    width = 2 * reach + 1
    row_count = framed_rows.shape[1] - 2 * reach
    col_count = framed_rows.shape[2]
    framed = jnp.pad(framed_rows, ((0, 0), (0, 0), (reach, reach), (0, 0)))
    total = jnp.zeros(
        (framed_rows.shape[0], row_count, col_count, framed_rows.shape[3]), jnp.float32
    )
    for row_off in range(width):
        for col_off in range(width):
            window = framed[:, row_off : row_off + row_count, col_off : col_off + col_count]
            total = total + window * kernel[row_off * width + col_off]
    return total


def kernel_terms(framed_rows, grad_map, reach):
    width = 2 * reach + 1
    row_count = grad_map.shape[1]
    col_count = grad_map.shape[2]
    framed = jnp.pad(framed_rows, ((0, 0), (0, 0), (reach, reach), (0, 0)))
    kernel_rows = []
    for row_off in range(width):
        for col_off in range(width):
            window = framed[:, row_off : row_off + row_count, col_off : col_off + col_count]
            kernel_rows.append(jnp.sum(window * grad_map, axis=(0, 1, 2)))
    return jnp.stack(kernel_rows)


GELU_C = 0.7978845608028654
GELU_A = 0.044715


def gelu_value(u):
    inner = GELU_C * (u + GELU_A * (u * u * u))
    return (0.5 * u) * (1.0 + jnp.tanh(inner))


def gelu_slope(u):
    square = u * u
    t = jnp.tanh(GELU_C * (u + GELU_A * (square * u)))
    return 0.5 * (1.0 + t) + (0.5 * GELU_C) * u * (1.0 - t * t) * (1.0 + (3.0 * GELU_A) * square)


def params(mebibytes):
    return pltpu.CompilerParams(vmem_limit_bytes=mebibytes * 1024 * 1024)


def mlp_forward_kernel(x_ref, up_w_ref, down_w_ref, own_ref, other_ref, up_ref, total):
    step = pl.program_id(0)
    width = x_ref.shape[1]
    up_w = up_w_ref[...].reshape(width, -1)
    down_w = down_w_ref[...].reshape(-1, width)
    up = jnp.dot(x_ref[...], up_w, preferred_element_type=jnp.float32)
    up_ref[...] = up.astype(jnp.bfloat16)
    act = gelu_value(up).astype(jnp.bfloat16)
    part = jnp.dot(act, down_w, preferred_element_type=jnp.float32)

    @pl.when(step == 0)
    def _():
        total[...] = part

    @pl.when(step > 0)
    def _():
        total[...] += part

    @pl.when(step == pl.num_programs(0) - 1)
    def _():
        rows = own_ref.shape[0]
        own_ref[...] = total[:rows]
        other_ref[...] = total[rows:].astype(jnp.bfloat16)


def mlp_backward_kernel(y_ref, up_ref, up_w_ref, down_w_ref, own_ref, other_ref, total):
    step = pl.program_id(0)
    width = y_ref.shape[1]
    up_w = up_w_ref[...].reshape(width, -1)
    down_w = down_w_ref[...].reshape(-1, width)
    act_grad = times_transposed(y_ref[...], down_w)
    slope = gelu_slope(up_ref[...].astype(jnp.float32))
    up_grad = (act_grad * slope).astype(jnp.bfloat16)
    part = times_transposed(up_grad, up_w)

    @pl.when(step == 0)
    def _():
        total[...] = part

    @pl.when(step > 0)
    def _():
        total[...] += part

    @pl.when(step == pl.num_programs(0) - 1)
    def _():
        rows = own_ref.shape[0]
        own_ref[...] = total[:rows]
        other_ref[...] = total[rows:].astype(jnp.bfloat16)


def mlp_specs(weights, half, block):
    devices, rows, width = weights.shape
    up_rows = width // devices
    per_set = width // block
    pieces = block // half
    return (
        pl.BlockSpec((devices, up_rows, block), lambda j: (0, j // per_set, j % per_set)),
        pl.BlockSpec((pieces, half, width), lambda j: (j, 1, 0)),
    )


def mlp_cost(rows, width, hidden):
    return pl.CostEstimate(
        flops=4 * rows * width * hidden,
        bytes_accessed=4 * width * hidden + 2 * rows * hidden + 8 * rows * width,
        transcendentals=rows * hidden,
    )


def mlp_forward(x, weights, half, block):
    rows, width = x.shape
    hidden = weights.shape[0] * half
    up_spec, down_spec = mlp_specs(weights, half, block)
    whole = lambda j: (0, 0)
    return pl.pallas_call(
        mlp_forward_kernel,
        grid=(hidden // block,),
        in_specs=[pl.BlockSpec((rows, width), whole), up_spec, down_spec],
        out_specs=[
            pl.BlockSpec((rows // 2, width), whole),
            pl.BlockSpec((rows // 2, width), whole),
            pl.BlockSpec((rows, block), lambda j: (0, j)),
        ],
        out_shape=[
            jax.ShapeDtypeStruct((rows // 2, width), jnp.float32),
            jax.ShapeDtypeStruct((rows // 2, width), jnp.bfloat16),
            jax.ShapeDtypeStruct((rows, hidden), jnp.bfloat16),
        ],
        scratch_shapes=[pltpu.VMEM((rows, width), jnp.float32)],
        compiler_params=params(56),
        cost_estimate=mlp_cost(rows, width, hidden),
        name="mlp_forward",
    )(x, weights, weights)


def mlp_backward(y, up, weights, half, block):
    rows, width = y.shape
    hidden = weights.shape[0] * half
    up_spec, down_spec = mlp_specs(weights, half, block)
    whole = lambda j: (0, 0)
    return pl.pallas_call(
        mlp_backward_kernel,
        grid=(hidden // block,),
        in_specs=[
            pl.BlockSpec((rows, width), whole),
            pl.BlockSpec((rows, block), lambda j: (0, j)),
            up_spec,
            down_spec,
        ],
        out_specs=[
            pl.BlockSpec((rows // 2, width), whole),
            pl.BlockSpec((rows // 2, width), whole),
        ],
        out_shape=[
            jax.ShapeDtypeStruct((rows // 2, width), jnp.float32),
            jax.ShapeDtypeStruct((rows // 2, width), jnp.bfloat16),
        ],
        scratch_shapes=[pltpu.VMEM((rows, width), jnp.float32)],
        compiler_params=params(56),
        cost_estimate=mlp_cost(rows, width, hidden),
        name="mlp_backward",
    )(y, up, weights, weights)


LANES = 128


def conv_chunk(framed, taps_ref, columns, reach, rows, cols):
    width = 2 * reach + 1
    totals = [None] * rows
    for col_off in range(width):
        taps = [taps_ref[pl.ds(row_off * width + col_off, 1), columns] for row_off in range(width)]
        for row in range(rows + 2 * reach):
            window = framed[row, pl.ds(8 - reach + col_off, cols), :]
            for row_off in range(width):
                target = row - row_off
                if 0 <= target < rows:
                    term = window * taps[row_off]
                    totals[target] = term if totals[target] is None else totals[target] + term
    return totals


def conv_norm_kernel(reach, map_ref, taps_ref, gain_ref, shift_ref, conv_ref, normed_ref, framed):
    rows, cols, channels = conv_ref.shape[1:]
    framed[:, :8] = jnp.zeros((framed.shape[0], 8, LANES), jnp.float32)
    framed[:, 8 + cols :] = jnp.zeros((framed.shape[0], 8, LANES), jnp.float32)

    @pl.loop(0, channels // LANES)
    def _(chunk):
        columns = pl.ds(pl.multiple_of(chunk * LANES, LANES), LANES)
        framed[:, 8 : 8 + cols] = map_ref[0, :, :, columns].astype(jnp.float32)
        totals = conv_chunk(framed, taps_ref, columns, reach, rows, cols)
        for row in range(rows):
            conv_ref[0, row, :, columns] = totals[row]

    @pl.loop(0, rows)
    def _(row):
        values = conv_ref[0, row]
        average = jnp.mean(values, axis=-1, keepdims=True)
        centred = values - average
        spread = jnp.mean(centred * centred, axis=-1, keepdims=True)
        normed = centred * lax.rsqrt(spread + EPS_CONV) * gain_ref[...] + shift_ref[...]
        normed_ref[0, row] = normed.astype(jnp.bfloat16)


def conv_add_kernel(reach, map_ref, taps_ref, base_ref, out_ref, framed):
    rows, cols, channels = out_ref.shape[1:]
    framed[:, :8] = jnp.zeros((framed.shape[0], 8, LANES), jnp.float32)
    framed[:, 8 + cols :] = jnp.zeros((framed.shape[0], 8, LANES), jnp.float32)

    @pl.loop(0, channels // LANES)
    def _(chunk):
        columns = pl.ds(pl.multiple_of(chunk * LANES, LANES), LANES)
        framed[:, 8 : 8 + cols] = map_ref[0, :, :, columns].astype(jnp.float32)
        totals = conv_chunk(framed, taps_ref, columns, reach, rows, cols)
        for row in range(rows):
            out_ref[0, row, :, columns] = totals[row] + base_ref[0, row, :, columns]


def conv_specs(framed_map, reach):
    images, framed_rows, cols, channels = framed_map.shape
    rows = framed_rows - 2 * reach
    per_image = lambda i: (i, 0, 0, 0)
    map_spec = pl.BlockSpec((1, framed_rows, cols, channels), per_image)
    out_spec = pl.BlockSpec((1, rows, cols, channels), per_image)
    taps_spec = pl.BlockSpec(((2 * reach + 1) ** 2, channels), lambda i: (0, 0))
    scratch = pltpu.VMEM((framed_rows, cols + 16, LANES), jnp.float32)
    cost = pl.CostEstimate(
        flops=2 * (2 * reach + 1) ** 2 * images * rows * cols * channels,
        bytes_accessed=10 * images * rows * cols * channels,
        transcendentals=0,
    )
    return (images, rows, cols, channels), map_spec, out_spec, taps_spec, scratch, cost


def conv_norm(framed_map, taps, gain, shift, reach):
    shape, map_spec, out_spec, taps_spec, scratch, cost = conv_specs(framed_map, reach)
    row_spec = pl.BlockSpec((1, shape[3]), lambda i: (0, 0))
    return pl.pallas_call(
        functools.partial(conv_norm_kernel, reach),
        grid=(shape[0],),
        in_specs=[map_spec, taps_spec, row_spec, row_spec],
        out_specs=[out_spec, out_spec],
        out_shape=[
            jax.ShapeDtypeStruct(shape, jnp.float32),
            jax.ShapeDtypeStruct(shape, jnp.bfloat16),
        ],
        scratch_shapes=[scratch],
        compiler_params=params(32),
        cost_estimate=cost,
        name="conv_norm",
    )(framed_map, taps, gain[None], shift[None])


def conv_add(framed_map, taps, base, reach):
    shape, map_spec, out_spec, taps_spec, scratch, cost = conv_specs(framed_map, reach)
    return pl.pallas_call(
        functools.partial(conv_add_kernel, reach),
        grid=(shape[0],),
        in_specs=[map_spec, taps_spec, out_spec],
        out_specs=out_spec,
        out_shape=jax.ShapeDtypeStruct(shape, jnp.float32),
        scratch_shapes=[scratch],
        compiler_params=params(32),
        cost_estimate=cost,
        name="conv_add",
    )(framed_map, taps, base)


def head_probs(q, k, mine, scale):
    own = jnp.where(mine, q, jnp.zeros_like(q))
    scores = times_transposed(own, k) * scale
    raised = jnp.exp(scores - jnp.max(scores, axis=-1, keepdims=True))
    return raised / jnp.sum(raised, axis=-1, keepdims=True)


def attention_kernel(head_size, q_ref, k_ref, v_ref, out_ref):
    q, k, v = q_ref[0], k_ref[0], v_ref[0]
    scale = head_size ** (-0.5)
    head_of = lax.broadcasted_iota(jnp.int32, q.shape, 1) // head_size
    result = jnp.zeros(q.shape, jnp.float32)
    for head in range(q.shape[1] // head_size):
        mine = head_of == head
        probs = head_probs(q, k, mine, scale).astype(jnp.bfloat16)
        result = jnp.where(mine, product(probs, v), result)
    out_ref[0] = result.astype(jnp.bfloat16)


def attention_grad_kernel(head_size, q_ref, k_ref, v_ref, g_ref, dq_ref, dk_ref, dv_ref):
    q, k, v, grad = q_ref[0], k_ref[0], v_ref[0], g_ref[0]
    scale = head_size ** (-0.5)
    head_of = lax.broadcasted_iota(jnp.int32, q.shape, 1) // head_size
    q_grad = k_grad = v_grad = jnp.zeros(q.shape, jnp.float32)
    for head in range(q.shape[1] // head_size):
        mine = head_of == head
        probs = head_probs(q, k, mine, scale)
        probs_grad = times_transposed(jnp.where(mine, grad, jnp.zeros_like(grad)), v)
        weighted = probs * probs_grad
        scores_grad = weighted - probs * jnp.sum(weighted, axis=-1, keepdims=True)
        scores_grad = scores_grad.astype(jnp.bfloat16)
        q_grad = jnp.where(mine, product(scores_grad, k), q_grad)
        k_grad = jnp.where(mine, row_contract(scores_grad, q), k_grad)
        v_grad = jnp.where(mine, row_contract(probs.astype(jnp.bfloat16), grad), v_grad)
    dq_ref[0] = (q_grad * scale).astype(jnp.bfloat16)
    dk_ref[0] = (k_grad * scale).astype(jnp.bfloat16)
    dv_ref[0] = v_grad.astype(jnp.bfloat16)


def attention_specs(by_head):
    images, tokens, width = by_head.shape
    pairs = width // 3 // LANES
    specs = [
        pl.BlockSpec((1, tokens, LANES), lambda i, h, kind=kind: (i, 0, kind * pairs + h))
        for kind in range(3)
    ]
    one = pl.BlockSpec((1, tokens, LANES), lambda i, h: (i, 0, h))
    out = jax.ShapeDtypeStruct((images, tokens, width // 3), jnp.bfloat16)
    return (images, pairs), specs, one, out


def attention(by_head, head_size):
    grid, specs, one, out = attention_specs(by_head)
    images, tokens, width = by_head.shape
    return pl.pallas_call(
        functools.partial(attention_kernel, head_size),
        grid=grid,
        in_specs=specs,
        out_specs=one,
        out_shape=out,
        compiler_params=params(48),
        cost_estimate=pl.CostEstimate(
            flops=4 * images * tokens * tokens * width // 3,
            bytes_accessed=3 * by_head.size,
            transcendentals=images * tokens * tokens * width // 3 // head_size,
        ),
        name="attention",
    )(by_head, by_head, by_head)


def attention_grad(by_head, grad, head_size):
    grid, specs, one, out = attention_specs(by_head)
    images, tokens, width = by_head.shape
    return pl.pallas_call(
        functools.partial(attention_grad_kernel, head_size),
        grid=grid,
        in_specs=specs + [one],
        out_specs=[one] * 3,
        out_shape=[out] * 3,
        compiler_params=params(48),
        cost_estimate=pl.CostEstimate(
            flops=10 * images * tokens * tokens * width // 3,
            bytes_accessed=5 * by_head.size,
            transcendentals=images * tokens * tokens * width // 3 // head_size,
        ),
        name="attention_grad",
    )(by_head, by_head, by_head, grad)


def exchange(values, axis, bit):
    size = lax.axis_size(axis)
    return lax.ppermute(values, axis, [(i, i ^ bit) for i in range(size)])


def bits_of(axis, lowest=1):
    size, bits = lax.axis_size(axis), []
    bit = lowest
    while bit < size:
        bits.append(bit)
        bit *= 2
    return bits


def gather_half(part, bits):
    held = part[None]
    for bit in bits:
        other = exchange(held, "dp", bit)
        held = jnp.concatenate([held, other], axis=0)
    return held.reshape((2,) * len(bits) + part.shape)


def gather_peers(part):
    bits = bits_of("dp", 2)
    count = len(bits)
    half = part.shape[1] // 2
    first = gather_half(part[:, :half], bits)
    second = gather_half(part[:, half:], bits[::-1])
    second = second.transpose(tuple(range(count))[::-1] + (count, count + 1))
    return jnp.concatenate([first, second], axis=-1).reshape(-1, part.shape[1])


def scatter_half(parts, bits):
    for bit in bits:
        other = exchange(parts[1].astype(jnp.bfloat16), "dp", bit)
        parts = parts[0].astype(jnp.float32) + other.astype(jnp.float32)
    return parts


def scatter_peers(total):
    bits = bits_of("dp", 2)
    count = len(bits)
    half = total.shape[1] // 2
    parts = total.reshape((2,) * count + (-1, total.shape[1]))
    first = scatter_half(parts[..., :half], bits[::-1])
    turned = parts[..., half:].transpose(tuple(range(count))[::-1] + (count, count + 1))
    second = scatter_half(turned, bits)
    return jnp.concatenate([first, second], axis=-1)


def scatter_blocks(values, axis, dim):
    size = lax.axis_size(axis)
    me = lax.axis_index(axis)
    bit, lead = 1, values.shape[:dim]
    shape = values.shape[dim + 1 :]
    while bit < size:
        blocks = values.shape[dim] // 2
        split = values.reshape(lead + (blocks, 2) + shape)
        mine = (me // bit) % 2
        keep = lax.dynamic_index_in_dim(split, mine, dim + 1, keepdims=False)
        send = lax.dynamic_index_in_dim(split, 1 - mine, dim + 1, keepdims=False)
        other = exchange(send.astype(jnp.bfloat16), axis, bit)
        values = keep + other.astype(jnp.float32)
        bit *= 2
    return values.reshape(lead + shape)


def body(
    vit_tokens,
    hires_map,
    norm1_gain,
    norm1_shift,
    qkv_weight,
    attn_weight,
    norm2_gain,
    norm2_shift,
    vit_fc1,
    vit_fc2,
    conv_kernel,
    conv_gain,
    conv_shift,
    conv_fc1,
    conv_fc2,
    layer_scale,
    adapter_weight,
    adapter_bias,
    adapter_kernel,
    adapter_gate,
    proj_fc1,
    proj_bias1,
    proj_fc2,
    proj_bias2,
    projected_cot,
    hires_cot,
):
    half_of = lax.rem(lax.axis_index("tile"), 2)
    width, channels = attn_weight.shape[1], conv_fc2.shape[1]

    def column_sets(matrix, count):
        sets = matrix.shape[1] // count
        return [matrix[:, i * count : (i + 1) * count] for i in range(sets)]

    def half_mlp(up_matrix, down_matrix):
        inner, outer = down_matrix.shape
        devices = lax.axis_size("dp")
        up_split = up_matrix.reshape(-1, devices, 2, inner // 2)
        up_half = lax.dynamic_index_in_dim(up_split, half_of, 2, keepdims=False)
        up_half = up_half.reshape(up_matrix.shape[0], -1)
        down_half = lax.dynamic_slice_in_dim(down_matrix, half_of * (inner // 2), inner // 2)
        return column_sets(up_half, outer) + [down_half]

    first_rows = jnp.concatenate(column_sets(qkv_weight, width) + [attn_weight])
    first_all = lax.all_gather(first_rows, "dp", axis=0, tiled=False)
    conv_all = lax.all_gather(
        jnp.concatenate(half_mlp(conv_fc1, conv_fc2)), "dp", axis=0, tiled=False
    )
    vit_rows_of = jnp.concatenate(half_mlp(vit_fc1, vit_fc2) + [adapter_weight])
    vit_all = lax.all_gather(vit_rows_of, "dp", axis=0, tiled=False)
    shard = attn_weight.shape[0]
    qkv_full = jnp.concatenate(
        [first_all[:, i * shard : (i + 1) * shard].reshape(-1, width) for i in range(3)], axis=1
    )
    attn_full = first_all[:, 3 * shard :].reshape(-1, width)
    adapter_full = vit_all[:, -adapter_weight.shape[0] :].reshape(-1, width)
    conv_half, vit_half = conv_fc2.shape[0] // 2, vit_fc2.shape[0] // 2
    conv_block, vit_block = max(384, conv_half), max(512, vit_half)
    dp_size, tile_size = lax.axis_size("dp"), lax.axis_size("tile")
    dp_index = lax.axis_index("dp")
    hidden = proj_fc2.shape[0]
    up_cols = lax.all_to_all(
        proj_fc1.reshape(-1, dp_size, hidden), "dp", split_axis=1, concat_axis=0, tiled=False
    ).reshape(-1, hidden)
    proj_up = jnp.concatenate([up_cols, exchange(up_cols, "dp", 1)], axis=1)
    proj_down = jnp.concatenate([proj_fc2, exchange(proj_fc2, "dp", 1)], axis=0)
    own_start, other_start = dp_index * hidden, (dp_index ^ 1) * hidden
    bias1_part = jnp.concatenate(
        [
            lax.dynamic_slice_in_dim(proj_bias1, own_start, hidden),
            lax.dynamic_slice_in_dim(proj_bias1, other_start, hidden),
        ]
    )
    out_grad = projected_cot.reshape(-1, projected_cot.shape[2])
    out_grads = gather_peers(out_grad)
    images = vit_tokens.shape[0]
    tok_rows = vit_tokens.shape[1]
    model_width = vit_tokens.shape[2]
    head_size = model_width // HEADS
    vit_rows = tok_rows // GV
    hires_rows = hires_map.shape[1]
    hires_cols = hires_map.shape[2]
    tokens_float = vit_tokens.astype(jnp.float32)
    normed_a, norm_a_back = jax.vjp(
        lambda values: layer_norm(values, norm1_gain, norm1_shift, EPS_VIT), tokens_float
    )
    qkv_all = product(normed_a.astype(jnp.bfloat16).reshape(-1, model_width), qkv_full).astype(
        jnp.bfloat16
    )
    qkv_all = qkv_all.reshape(images, tok_rows, 3 * model_width)
    heads_here = HEADS // tile_size
    seq_tokens = tok_rows * tile_size

    def to_heads(values, kinds):
        split = values.reshape(images, tok_rows, kinds, tile_size, heads_here * head_size)
        moved = lax.all_to_all(split, "tile", split_axis=3, concat_axis=1, tiled=False)
        return moved.reshape(images, seq_tokens, -1)

    def from_heads(values, kinds):
        split = values.reshape(images, tile_size, tok_rows, kinds, heads_here * head_size)
        moved = lax.all_to_all(split, "tile", split_axis=1, concat_axis=3, tiled=False)
        return moved.reshape(images, tok_rows, kinds * model_width)

    by_head = to_heads(qkv_all, 3)
    attended = from_heads(attention(by_head, head_size), 1).reshape(-1, model_width)
    hidden_a = tokens_float + product(attended, attn_full).reshape(images, tok_rows, model_width)
    normed_b, norm_b_back = jax.vjp(
        lambda values: layer_norm(values, norm2_gain, norm2_shift, EPS_VIT), hidden_a
    )
    vit_own, vit_other, up_a = mlp_forward(
        with_partner(normed_b.astype(jnp.bfloat16).reshape(-1, model_width)),
        vit_all,
        vit_half,
        vit_block,
    )
    vit_out = hidden_a + (vit_own + exchange(vit_other, "tile", 1).astype(jnp.float32)).reshape(
        images, tok_rows, model_width
    )
    hires_float = hires_map.astype(jnp.float32)
    hires_framed = padded(hires_map, (("tile", 1),), 3)
    conv_in, normed_c = conv_norm(hires_framed, conv_kernel, conv_gain, conv_shift, 3)
    _, norm_c_back = jax.vjp(
        lambda values: layer_norm(values, conv_gain, conv_shift, EPS_CONV), conv_in
    )
    conv_own, conv_other, up_c = mlp_forward(
        with_partner(normed_c.reshape(-1, channels)), conv_all, conv_half, conv_block
    )
    refined = hires_float + layer_scale * (
        conv_own + exchange(conv_other, "tile", 1).astype(jnp.float32)
    ).reshape(hires_map.shape)
    hires_out = refined.astype(jnp.bfloat16)
    pool = jnp.kron(pool_matrix(vit_rows, hires_rows), pool_matrix(GV, hires_cols))
    pool = pool.astype(jnp.bfloat16)
    pooled_low = jnp.einsum(
        "pr,irc->ipc",
        pool,
        hires_out.reshape(images, -1, channels),
        preferred_element_type=jnp.float32,
    )
    pooled_low = pooled_low.astype(jnp.bfloat16).reshape(-1, channels)
    adapted = (product(pooled_low, adapter_full) + adapter_bias).astype(jnp.bfloat16)
    adapted = adapted.reshape(images, vit_rows, GV, model_width)
    adapted_framed = padded(adapted, (("tile", 1),), 1)
    mixed_map = depthwise_rows(adapted_framed, adapter_kernel, 1).reshape(
        images, tok_rows, model_width
    )
    gate_value = jnp.tanh(adapter_gate)
    merged = vit_out + gate_value * mixed_map
    merged_low = merged.astype(jnp.bfloat16).reshape(-1, model_width)
    merged_all = gather_peers(merged_low)
    pre_act = product(merged_all, proj_up) + bias1_part
    act_p, gelu_p_back = jax.vjp(jax.nn.gelu, pre_act)
    act_p_low = act_p.astype(jnp.bfloat16)
    projected = (
        (scatter_peers(product(act_p_low, proj_down).astype(jnp.bfloat16)) + proj_bias2)
        .astype(jnp.bfloat16)
        .reshape(images, tok_rows, -1)
    )
    bias2_grad = jnp.sum(out_grad.astype(jnp.float32), axis=0)
    pre_grad = gelu_p_back(times_transposed(out_grads, proj_down))[0].astype(jnp.bfloat16)
    merged_grad = scatter_peers(
        times_transposed(pre_grad, proj_up).astype(jnp.bfloat16)
    ).reshape(images, tok_rows, model_width)
    fc2_part = row_contract(act_p_low, out_grads)
    fc2_part = fc2_part[:hidden] + exchange(
        fc2_part[hidden:].astype(jnp.bfloat16), "dp", 1
    ).astype(jnp.float32)
    fc2_grad = scatter_blocks(
        fc2_part.reshape(tile_size, -1, fc2_part.shape[1]), "tile", 0
    )
    fc1_part = row_contract(merged_all, pre_grad)
    fc1_part = fc1_part[:, :hidden] + exchange(
        fc1_part[:, hidden:].astype(jnp.bfloat16), "dp", 1
    ).astype(jnp.float32)
    fc1_part = scatter_blocks(
        fc1_part.reshape(dp_size, tile_size, -1, hidden), "tile", 1
    )
    fc1_grad = lax.all_to_all(
        fc1_part.astype(jnp.bfloat16), "dp", split_axis=0, concat_axis=1, tiled=False
    )
    fc1_grad = fc1_grad.reshape(fc1_grad.shape[0], -1).astype(jnp.float32)
    bias1_sum = jnp.sum(pre_grad.astype(jnp.float32), axis=0)
    bias1_grad = jnp.zeros_like(proj_bias1)
    bias1_grad = lax.dynamic_update_slice_in_dim(bias1_grad, bias1_sum[:hidden], own_start, 0)
    bias1_grad = lax.dynamic_update_slice_in_dim(bias1_grad, bias1_sum[hidden:], other_start, 0)
    gate_grad = jnp.sum(merged_grad * mixed_map, axis=(0, 1)) * (1.0 - gate_value * gate_value)
    mixed_grad = (gate_value * merged_grad).reshape(images, vit_rows, GV, model_width)
    mixed_framed = padded(mixed_grad.astype(jnp.bfloat16), (("tile", 1),), 1).astype(
        mixed_grad.dtype
    )
    kernel_grad = kernel_terms(adapted_framed, mixed_grad, 1)
    adapted_grad = (
        depthwise_rows(mixed_framed, adapter_kernel[::-1], 1)
        .astype(jnp.bfloat16)
        .reshape(-1, model_width)
    )
    bias_a_grad = jnp.sum(adapted_grad.astype(jnp.float32), axis=0)
    adapter_part = row_contract(pooled_low, adapted_grad)
    adapter_part = adapter_part.reshape(dp_size, tile_size, -1, model_width)
    adapter_grad = scatter_blocks(scatter_blocks(adapter_part, "dp", 0), "tile", 0)
    pooled_grad = times_transposed(adapted_grad, adapter_full).astype(jnp.bfloat16)
    unpooled = jnp.einsum(
        "pr,ipc->irc",
        pool,
        pooled_grad.reshape(images, -1, channels),
        preferred_element_type=jnp.float32,
    ).reshape(hires_map.shape)
    refined_grad = hires_cot.astype(jnp.float32) + unpooled
    branch_grad = (layer_scale * refined_grad).astype(jnp.bfloat16).reshape(-1, channels)
    conv_own, conv_other = mlp_backward(
        with_partner(branch_grad), up_c, conv_all, conv_half, conv_block
    )
    normed_c_grad = conv_own + exchange(conv_other, "tile", 1).astype(jnp.float32)
    conv_in_grad = norm_c_back(normed_c_grad.reshape(hires_map.shape))[0]
    conv_framed = padded(conv_in_grad.astype(jnp.bfloat16), (("tile", 1),), 3)
    hires_grad = conv_add(conv_framed, conv_kernel[::-1], refined_grad, 3)
    down_grad = merged_grad.astype(jnp.bfloat16).reshape(-1, model_width)
    vit_own, vit_other = mlp_backward(
        with_partner(down_grad), up_a, vit_all, vit_half, vit_block
    )
    normed_b_grad = vit_own + exchange(vit_other, "tile", 1).astype(jnp.float32)
    hidden_grad = merged_grad + norm_b_back(normed_b_grad.reshape(merged_grad.shape))[0]
    attn_grad = hidden_grad.astype(jnp.bfloat16).reshape(-1, model_width)
    attended_grad = to_heads(
        times_transposed(attn_grad, attn_full)
        .astype(jnp.bfloat16)
        .reshape(images, tok_rows, model_width),
        1,
    )
    qkv_grad = jnp.stack(attention_grad(by_head, attended_grad, head_size), axis=2)
    qkv_grad = from_heads(qkv_grad, 3).reshape(-1, 3 * model_width)
    tokens_grad = (
        hidden_grad
        + norm_a_back(times_transposed(qkv_grad, qkv_full).reshape(images, tok_rows, model_width))[
            0
        ]
    )
    bias2_grad, bias1_grad, bias_a_grad, kernel_grad, gate_grad = lax.psum(
        (bias2_grad, bias1_grad, bias_a_grad, kernel_grad, gate_grad), ("dp", "tile")
    )
    return (
        projected,
        hires_out,
        tokens_grad,
        hires_grad,
        adapter_grad,
        bias_a_grad,
        kernel_grad,
        gate_grad,
        fc1_grad,
        bias1_grad,
        fc2_grad,
        bias2_grad,
    )


def solution(mesh):
    in_specs = (
        P("dp", "tile", None),
        P("dp", "tile", None, None),
        P(),
        P(),
        P("dp", None),
        P("dp", None),
        P(),
        P(),
        P("dp", None),
        P("dp", None),
        P(),
        P(),
        P(),
        P("dp", None),
        P("dp", None),
        P(),
        P("dp", None),
        P(),
        P(),
        P(),
        P("dp", None),
        P(),
        P("dp", None),
        P(),
        P("dp", "tile", None),
        P("dp", "tile", None, None),
    )
    out_specs = (
        P("dp", "tile", None),
        P("dp", "tile", None, None),
        P("dp", "tile", None),
        P("dp", "tile", None, None),
        P(("dp", "tile"), None),
        P(),
        P(),
        P(),
        P(("dp", "tile"), None),
        P(),
        P(("dp", "tile"), None),
        P(),
    )
    return jax.shard_map(body, mesh=mesh, in_specs=in_specs, out_specs=out_specs, check_vma=False)
```
